32 devices in a mesh: dp: 8 (over z, y), fsdp: 4 (over x, core).
Axes of the slice: x: 2, y: 2, z: 4, core: 2. Of those that a mesh axis runs over, the one named last changes fastest.
Arguments:
- features: bfloat16 [32, 8, 256, 128], P(('dp', 'fsdp')), may hold values from -60 to 60, as said below
- pick_index: int32 [32, 8, 2], P(('dp', 'fsdp')), may hold values from 0 to 255
- good_channel: int32 [32, 8], P(('dp', 'fsdp')), may hold values 0 or 1
- conv_weight: bfloat16 [1152, 128], P(None, 'fsdp'), may hold values from -0.1875 to 0.1875
- conv_bias: bfloat16 [1, 128], P(None, 'fsdp'), may hold values from -3 to 3
- head_weight: bfloat16 [2, 128], P(None, 'fsdp'), may hold values from -0.5 to 0.5
- head_bias: float32 [2], replicated, may hold values from -2 to 2
Outputs:
- grad_conv_weight: float32 [1152, 128], P('dp', 'fsdp')
- grad_conv_bias: float32 [1, 128], P(None, 'fsdp')
- grad_head_weight: float32 [2, 128], P(None, 'fsdp')
- grad_head_bias: float32 [2], replicated
- grad_features: bfloat16 [32, 8, 256, 128], P(('dp', 'fsdp'))
The draws below stay inside these ranges and needn't reach their ends.
Inputs may be any that keep to these rules, and one draw needn't show every extreme that they name: `features`: real-valued feature maps.
All inputs are finite; a program needn't handle non-finite values. No bound on the sum of `good_channel` on one device may be relied on, other than what follows from the above.
Results may differ from the reference program's by a relative error of at most 0.007.
Values may be sent and summed in bfloat16 or wider, within the bound.
A program may use at most 64 MiB of HBM per device.

```python
import jax
import jax.numpy as jnp
from jax import lax

C = 128
ROWS = 8
SAMPLES = 256
PATCH_DEV = 1
SIGMA = 20
PATCHES = 32
N_DP = 8
N_FSDP = 4


def draw_features(key, part):
    patch_ids = jnp.arange(PATCHES, dtype=jnp.int32)
    device_ids = patch_ids // PATCH_DEV
    cycle_pos = (device_ids // N_FSDP).astype(jnp.float32) / max(N_DP - 1, 1)
    member_pos = (device_ids % N_FSDP).astype(jnp.float32) / max(N_FSDP - 1, 1)
    base = jnp.clip(jax.random.normal(key, (PATCHES, ROWS, SAMPLES, C), jnp.float32), -6.0, 6.0)
    scale = 0.03 * jnp.exp(cycle_pos * jnp.log(100.0)) * jnp.exp(member_pos * jnp.log(3.0))
    return (base * scale[:, None, None, None]).astype(jnp.bfloat16)


def with_ends(entries, own_key, least, largest):
    spot = [jax.random.randint(jax.random.fold_in(own_key, axis), (), 0, length) for axis, length in enumerate(entries.shape)]
    widest = entries.shape.index(max(entries.shape))
    neighbour = spot[:widest] + [(spot[widest] + 1) % entries.shape[widest]] + spot[widest + 1:]
    return entries.at[tuple(spot)].set(least).at[tuple(neighbour)].set(largest)


def block_levels(own_key, dims, shards, low, largest):
    def one(dim, blocks):
        draws = jax.random.uniform(jax.random.fold_in(jax.random.fold_in(own_key, 6), dim), (blocks,), jnp.float32, low / len(shards), largest / len(shards))
        return jnp.repeat(jnp.exp(draws), dims[dim] // blocks).reshape((-1,) + (1,) * (len(dims) - dim - 1))

    factor_of = one(*shards[0])
    for cut in shards[1:]:
        factor_of = factor_of * one(*cut)
    return factor_of


def gaussian(rng, extent, scale, reach, cuts=(), held_as=jnp.bfloat16):
    loudness = block_levels(rng, extent, cuts, -0.22, 0.18) if cuts else 1.0
    result = jax.random.normal(rng, extent, jnp.float32) * scale * loudness
    return jnp.minimum(jnp.maximum(result, -reach), reach).astype(held_as)


def setup_inputs(seed: int = 0) -> dict:
    keys = jax.random.split(jax.random.key(seed), 8)
    features = draw_features(jax.random.fold_in(keys[7], 71), 0)
    pick_index = with_ends(jax.random.randint(keys[1], (PATCHES, ROWS, 2), 0, SAMPLES), jax.random.fold_in(keys[1], 1), 0, SAMPLES - 1).astype(jnp.int32)
    good_channel = with_ends((jax.random.randint(keys[2], (PATCHES, ROWS), 0, 8) < 7).astype(jnp.int32), jax.random.fold_in(keys[2], 1), 0, 1)
    conv_weight = gaussian(keys[3], (9 * C, C), (9 * C) ** -0.5, 0.1875, ((1, 4),))
    conv_bias = gaussian(keys[4], (1, C), 0.5, 3.0, ((1, 4),))
    head_weight = gaussian(keys[5], (2, C), C ** -0.5, 0.5, ((1, 4),))
    head_bias = jnp.clip(jax.random.uniform(keys[6], (2,), jnp.float32, -2.0, 2.0), -2.0, 2.0)
    return {"features": features, "pick_index": pick_index, "good_channel": good_channel, "conv_weight": conv_weight, "conv_bias": conv_bias, "head_weight": head_weight, "head_bias": head_bias}


def local_grads(features, pick_index, good_channel, conv_weight, conv_bias, head_weight, head_bias):
    patch_count, row_count, sample_count, width = features.shape
    cells = patch_count * row_count * sample_count
    padded = jnp.pad(features, ((0, 0), (1, 1), (1, 1), (0, 0)))
    preact = jnp.zeros((cells, width), jnp.float32) + conv_bias.astype(jnp.float32)
    shifted = []
    for tap_index in range(9):
        offset_row = tap_index // 3
        offset_col = tap_index % 3
        window = padded[:, offset_row:offset_row + row_count, offset_col:offset_col + sample_count, :].reshape(cells, width)
        shifted.append(window)
        preact = preact + jnp.dot(window, conv_weight[tap_index * width:(tap_index + 1) * width], preferred_element_type=jnp.float32)
    gate_value = jax.nn.sigmoid(preact)
    hidden = (preact * gate_value).astype(jnp.bfloat16)
    slope_term = gate_value * (1.0 + preact * (1.0 - gate_value))
    logits = jnp.einsum("kc,nc->kn", head_weight, hidden, preferred_element_type=jnp.float32) + head_bias[:, None]
    positions = jnp.arange(sample_count, dtype=jnp.float32)
    arrival = jnp.transpose(pick_index, (2, 0, 1)).astype(jnp.float32)[..., None]
    target = jnp.exp(-(positions - arrival) ** 2 / (2.0 * SIGMA * SIGMA)).reshape(2, cells)
    usable = jnp.broadcast_to(good_channel.astype(jnp.float32)[:, :, None], (patch_count, row_count, sample_count)).reshape(1, cells)
    dlogit = (usable * (jax.nn.sigmoid(logits) - target)).astype(jnp.bfloat16)
    grad_head_weight = jnp.dot(dlogit, hidden, preferred_element_type=jnp.float32)
    grad_head_bias = jnp.sum(dlogit.astype(jnp.float32), axis=1)
    dact = jnp.einsum("kn,kc->nc", dlogit, head_weight, preferred_element_type=jnp.float32)
    dpre = (dact * slope_term).astype(jnp.bfloat16)
    grad_conv_bias = jnp.sum(dpre.astype(jnp.float32), axis=0)[None, :]
    blocks = [jnp.einsum("nc,nd->cd", window, dpre, preferred_element_type=jnp.float32) for window in shifted]
    grad_conv_weight = jnp.concatenate(blocks, axis=0)
    dpad = jnp.pad(dpre.reshape(patch_count, row_count, sample_count, width), ((0, 0), (1, 1), (1, 1), (0, 0)))
    back = jnp.zeros((cells, width), jnp.float32)
    for tap_index in range(9):
        offset_row = tap_index // 3
        offset_col = tap_index % 3
        window = dpad[:, 2 - offset_row:2 - offset_row + row_count, 2 - offset_col:2 - offset_col + sample_count, :].reshape(cells, width)
        back = back + jnp.einsum("nd,cd->nc", window, conv_weight[tap_index * width:(tap_index + 1) * width], preferred_element_type=jnp.float32)
    grad_features = back.astype(jnp.bfloat16).reshape(patch_count, row_count, sample_count, width)
    return grad_conv_weight, grad_conv_bias, grad_head_weight, grad_head_bias, grad_features


def reference(features, pick_index, good_channel, conv_weight, conv_bias, head_weight, head_bias):
    width = features.shape[-1]

    def one_patch(carry, items):
        patch, picks, usable = items
        parts = local_grads(patch[None], picks[None], usable[None], conv_weight, conv_bias, head_weight, head_bias)
        carry = (carry[0] + parts[0], carry[1] + parts[1], carry[2] + parts[2], carry[3] + parts[3])
        return carry, parts[4][0]

    start = (jnp.zeros((9 * width, width), jnp.float32), jnp.zeros((1, width), jnp.float32),
             jnp.zeros((2, width), jnp.float32), jnp.zeros((2,), jnp.float32))
    totals, grad_features = lax.scan(one_patch, start, (features, pick_index, good_channel))
    return totals[0], totals[1], totals[2], totals[3], grad_features
```

```python
import functools

import jax
import jax.numpy as jnp
from jax import lax
from jax.experimental import pallas as pl
from jax.experimental.pallas import tpu as pltpu
from jax.sharding import PartitionSpec as P

SIGMA = 20
MESH = pl.DeviceIdType.MESH
AUX = 8
NT = (((1,), (1,)), ((), ()))
TN = (((0,), (0,)), ((), ()))
f32 = jnp.float32
bf16 = jnp.bfloat16


def kernel(
    n_dp,
    n_fsdp,
    rows,
    samples,
    owned,
    span,
    feat_ref,
    pick_ref,
    good_ref,
    cw_ref,
    cb_ref,
    hw_ref,
    hb_ref,
    gw_ref,
    gb_ref,
    gh_ref,
    ghb_ref,
    gf_ref,
    wt,
    wn,
    wb,
    nat,
    xc,
    dc,
    dt,
    gs,
    recv1,
    acc,
    s2,
    recv2,
    g_send,
    g_recv,
    r1_send,
    r1_recv,
    r2_send,
    r2_recv,
):
    C = wt.shape[0]
    K3 = 3 * C
    own = C // n_fsdp
    cells = rows * samples
    my_d = lax.axis_index("dp")
    my_f = lax.axis_index("fsdp")
    chunks = [(K3 * a, K3) for a in range(3)] + [(3 * K3, C)]
    mine = pl.ds(pl.multiple_of(my_f * own, own), own)

    barrier = pltpu.get_barrier_semaphore()
    for k in range(1, n_fsdp):
        pl.semaphore_signal(
            barrier, inc=1, device_id=(my_d, lax.rem(my_f + k, n_fsdp)), device_id_type=MESH
        )
    for k in range(1, n_dp):
        pl.semaphore_signal(
            barrier, inc=1, device_id=(lax.rem(my_d + k, n_dp), my_f), device_id_type=MESH
        )

    nat[...] = jnp.zeros_like(nat)
    nat[0:2, 0:own] = hw_ref[...].astype(f32)
    nat[2:3, 0:own] = cb_ref[...].astype(f32)
    wt[mine, 0 : 3 * K3] = cw_ref[...]
    wt[mine, 3 * K3 : 3 * K3 + C] = jnp.transpose(nat[...])[0:own, :].astype(bf16)

    pl.semaphore_wait(barrier, (n_fsdp - 1) + (n_dp - 1))

    gathers = []
    for q in (3, 0, 1, 2):
        start, size = chunks[q]
        for k in range(1, n_fsdp):
            copy = pltpu.make_async_remote_copy(
                src_ref=wt.at[mine, pl.ds(start, size)],
                dst_ref=wt.at[mine, pl.ds(start, size)],
                send_sem=g_send.at[k - 1, q],
                recv_sem=g_recv.at[k - 1, q],
                device_id=(my_d, lax.rem(my_f + k, n_fsdp)),
                device_id_type=MESH,
            )
            copy.start()
            gathers.append(copy)

    pad = jnp.zeros((samples, K3), bf16)
    for ref in (xc, dc):
        ref[0:samples, :] = pad
        ref[(rows + 1) * samples : (rows + 2) * samples, :] = pad
    spot = lax.broadcasted_iota(jnp.int32, (samples, C), 0)
    for i in range(rows):
        at = slice((i + 1) * samples, (i + 2) * samples)
        block = feat_ref[i * samples : (i + 1) * samples, :]
        wide = block.astype(f32)
        before = jnp.where(spot == 0, 0.0, pltpu.roll(wide, 1, 0))
        after = jnp.where(spot == samples - 1, 0.0, pltpu.roll(wide, samples - 1, 0))
        xc[at, 0:C] = before.astype(bf16)
        xc[at, C : 2 * C] = block
        xc[at, 2 * C : K3] = after.astype(bf16)

    for copy in gathers:
        copy.wait_recv()

    for t in range(9):
        part = wt[:, t * C : (t + 1) * C]
        wb[t * C : (t + 1) * C, :] = part
        wn[t * C : (t + 1) * C, :] = jnp.transpose(part.astype(f32)).astype(bf16)
    small = jnp.transpose(wt[:, 3 * K3 : 3 * K3 + C].astype(f32))
    head = small[0:16].astype(bf16)
    bias = small[2:3]

    sub = lax.broadcasted_iota(jnp.int32, (16, samples), 0)
    lane = lax.broadcasted_iota(jnp.int32, (16, samples), 1).astype(f32)
    head_bias = jnp.where(sub == 0, hb_ref[0], hb_ref[1])
    grad_head = jnp.zeros((16, C), f32)
    grad_hbias = jnp.zeros((16, samples), f32)
    grad_bias = jnp.zeros((1, C), f32)
    for i in range(rows):
        preact = bias
        for a in range(3):
            preact = preact + jnp.dot(
                xc[(i + a) * samples : (i + a + 1) * samples, :],
                wn[a * K3 : (a + 1) * K3, :],
                preferred_element_type=f32,
            )
        gate = jax.nn.sigmoid(preact)
        hidden = (preact * gate).astype(bf16)
        slope = gate * (1.0 + preact * (1.0 - gate))
        logits = lax.dot_general(head, hidden, NT, preferred_element_type=f32) + head_bias
        arrival = jnp.where(sub == 0, pick_ref[0, i], pick_ref[1, i]).astype(f32)
        gap = lane - arrival
        target = jnp.exp(-(gap * gap) / (2.0 * SIGMA * SIGMA))
        usable = jnp.where(sub < 2, good_ref[0, i].astype(f32), 0.0)
        dlogit = (usable * (jax.nn.sigmoid(logits) - target)).astype(bf16)
        grad_head = grad_head + jnp.dot(dlogit, hidden, preferred_element_type=f32)
        grad_hbias = grad_hbias + dlogit.astype(f32)
        dact = lax.dot_general(dlogit, head, TN, preferred_element_type=f32)
        dpre = (dact * slope).astype(bf16)
        wide = dpre.astype(f32)
        grad_bias = grad_bias + jnp.sum(wide, axis=0, keepdims=True)
        dt[:, i * samples : (i + 1) * samples] = jnp.transpose(wide).astype(bf16)
        before = jnp.where(spot == 0, 0.0, pltpu.roll(wide, 1, 0))
        after = jnp.where(spot == samples - 1, 0.0, pltpu.roll(wide, samples - 1, 0))
        at = slice((i + 1) * samples, (i + 2) * samples)
        dc[at, 0:C] = after.astype(bf16)
        dc[at, C : 2 * C] = dpre
        dc[at, 2 * C : K3] = before.astype(bf16)

    def scatter(q):
        start, size = chunks[q]
        for k in range(1, n_fsdp):
            peer = lax.rem(my_f + k, n_fsdp)
            copy = pltpu.make_async_remote_copy(
                src_ref=gs.at[pl.ds(pl.multiple_of(peer * own, own), own), pl.ds(start, size)],
                dst_ref=recv1.at[k - 1, :, pl.ds(start, size)],
                send_sem=r1_send.at[k - 1, q],
                recv_sem=r1_recv.at[k - 1, q],
                device_id=(my_d, peer),
                device_id_type=MESH,
            )
            copy.start()
            firsts[q].append(copy)

    def split(value):
        high = value.astype(bf16).astype(f32)
        return high, value - high

    firsts = [[], [], [], []]
    for a in range(3):
        grads = jnp.dot(
            dt[...], xc[a * samples : a * samples + cells, :], preferred_element_type=f32
        )
        gs[:, a * K3 : (a + 1) * K3] = grads.astype(bf16)
        scatter(a)
    hsum = jnp.sum(grad_hbias, axis=1, keepdims=True)
    sub8 = lax.broadcasted_iota(jnp.int32, (AUX, C), 0)
    rest = jnp.where(sub8 == 2, grad_bias, jnp.where(sub8 == 3, hsum[0:1], hsum[1:2]))
    rest = jnp.where(sub8 < 2, grad_head[0:AUX], jnp.where(sub8 < 5, rest, 0.0))
    high, low = split(rest)
    nat[...] = jnp.zeros_like(nat)
    nat[0:AUX, :] = high
    nat[AUX : 2 * AUX, :] = low
    gs[:, 3 * K3 : 3 * K3 + C] = jnp.transpose(nat[...]).astype(bf16)
    scatter(3)

    for i in range(rows):
        back = jnp.zeros((samples, C), f32)
        for a in range(3):
            back = back + jnp.dot(
                dc[(i + 2 - a) * samples : (i + 3 - a) * samples, :],
                wb[a * K3 : (a + 1) * K3, :],
                preferred_element_type=f32,
            )
        gf_ref[i * samples : (i + 1) * samples, :] = back.astype(bf16)

    for q in range(4):
        start, size = chunks[q]
        total = gs[mine, start : start + size].astype(f32)
        for k in range(1, n_fsdp):
            firsts[q][k - 1].wait_recv()
            total = total + recv1[k - 1, :, start : start + size].astype(f32)
        acc[:, start : start + size] = total
    acc[:, 3 * K3 + C :] = jnp.zeros((own, acc.shape[1] - 3 * K3 - C), f32)

    column = lax.broadcasted_iota(jnp.int32, (own, span), 1)
    small = acc[:, 3 * K3 : 3 * K3 + span]
    small = small + pltpu.roll(small, span - AUX, 1)
    high, low = split(small)
    high = pltpu.roll(high, owned, 1)
    low = pltpu.roll(low, owned + AUX, 1)
    small = jnp.where(column < owned + AUX, high, jnp.where(column < owned + 2 * AUX, low, 0.0))
    for d in range(n_dp):
        base = owned * d // 128 * 128
        piece = acc[:, base : base + span + 128]
        if owned * d > base:
            piece = pltpu.roll(piece, span + 128 - (owned * d - base), 1)
        s2[d] = jnp.where(column < owned, piece[:, 0:span], small).astype(bf16)

    seconds = []
    for k in range(1, n_dp):
        peer = lax.rem(my_d + k, n_dp)
        copy = pltpu.make_async_remote_copy(
            src_ref=s2.at[peer],
            dst_ref=recv2.at[k - 1],
            send_sem=r2_send.at[k - 1],
            recv_sem=r2_recv.at[k - 1],
            device_id=(peer, my_f),
            device_id_type=MESH,
        )
        copy.start()
        seconds.append(copy)
    total = s2[my_d].astype(f32)
    for k in range(1, n_dp):
        seconds[k - 1].wait_recv()
        total = total + recv2[k - 1].astype(f32)
    gw_ref[...] = total[:, 0:owned]
    small = pltpu.roll(total, span - owned, 1)
    small = small + pltpu.roll(small, span - AUX, 1)
    nat[0:own, :] = small[:, 0:C]
    ghb_ref[...] = small[0:1, 3:5]
    turned = jnp.transpose(nat[...])
    gh_ref[...] = turned[0:2, 0:own]
    gb_ref[...] = turned[2:3, 0:own]

    for copies in [gathers, *firsts, seconds]:
        for copy in copies:
            copy.wait_send()


def on_device(n_dp, n_fsdp, features, pick_index, good_channel, conv_weight, conv_bias, head_weight, head_bias):
    _, rows, samples, C = features.shape
    cells = rows * samples
    K9 = conv_weight.shape[0]
    own = conv_weight.shape[1]
    owned = K9 // n_dp
    span = -(-(owned + 2 * AUX) // 128) * 128
    vmem = pl.BlockSpec(memory_space=pltpu.VMEM)
    smem = pl.BlockSpec(memory_space=pltpu.SMEM)
    dma = pltpu.SemaphoreType.DMA
    gw, gb, gh, ghb, gf = pl.pallas_call(
        functools.partial(kernel, n_dp, n_fsdp, rows, samples, owned, span),
        out_shape=(
            jax.ShapeDtypeStruct((own, owned), f32),
            jax.ShapeDtypeStruct((1, own), f32),
            jax.ShapeDtypeStruct((2, own), f32),
            jax.ShapeDtypeStruct((1, 2), f32),
            jax.ShapeDtypeStruct((cells, C), bf16),
        ),
        in_specs=[vmem, smem, smem, vmem, vmem, vmem, smem],
        out_specs=(vmem,) * 5,
        scratch_shapes=[
            pltpu.VMEM((C, K9 + C), bf16),
            pltpu.VMEM((K9, C), bf16),
            pltpu.VMEM((K9, C), bf16),
            pltpu.VMEM((C, C), f32),
            pltpu.VMEM(((rows + 2) * samples, 3 * C), bf16),
            pltpu.VMEM(((rows + 2) * samples, 3 * C), bf16),
            pltpu.VMEM((C, cells), bf16),
            pltpu.VMEM((C, K9 + C), bf16),
            pltpu.VMEM((n_fsdp - 1, own, K9 + C), bf16),
            pltpu.VMEM((own, K9 + span + 128), f32),
            pltpu.VMEM((n_dp, own, span), bf16),
            pltpu.VMEM((n_dp - 1, own, span), bf16),
            dma((n_fsdp - 1, 4)),
            dma((n_fsdp - 1, 4)),
            dma((n_fsdp - 1, 4)),
            dma((n_fsdp - 1, 4)),
            dma((n_dp - 1,)),
            dma((n_dp - 1,)),
        ],
        compiler_params=pltpu.CompilerParams(
            collective_id=0, has_side_effects=True, vmem_limit_bytes=48 * 1024 * 1024
        ),
        cost_estimate=pl.CostEstimate(
            flops=6 * cells * K9 * C, bytes_accessed=4 * cells * C, transcendentals=2 * cells * C
        ),
    )(
        features.reshape(cells, C),
        jnp.transpose(pick_index[0]),
        good_channel,
        jnp.transpose(conv_weight),
        conv_bias,
        head_weight,
        head_bias,
    )
    return jnp.transpose(gw), gb, gh, ghb.reshape(2), gf.reshape(features.shape)


def solution(mesh):
    return jax.shard_map(
        functools.partial(on_device, mesh.shape["dp"], mesh.shape["fsdp"]),
        mesh=mesh,
        in_specs=(
            P(("dp", "fsdp"), None, None, None),
            P(("dp", "fsdp"), None, None),
            P(("dp", "fsdp"), None),
            P(None, "fsdp"),
            P(None, "fsdp"),
            P(None, "fsdp"),
            P(),
        ),
        out_specs=(
            P("dp", "fsdp"),
            P(None, "fsdp"),
            P(None, "fsdp"),
            P(),
            P(("dp", "fsdp"), None, None, None),
        ),
        check_vma=False,
    )
```

```python
import functools

import jax
import jax.numpy as jnp
from jax import lax
from jax.experimental import pallas as pl
from jax.experimental.pallas import tpu as pltpu
from jax.sharding import PartitionSpec as P

SIGMA = 20
MESH = pl.DeviceIdType.MESH
AUX = 8
NT = (((1,), (1,)), ((), ()))
TN = (((0,), (0,)), ((), ()))
f32 = jnp.float32
bf16 = jnp.bfloat16


def kernel(
    n_dp,
    n_fsdp,
    rows,
    samples,
    owned,
    span,
    feat_ref,
    pick_ref,
    good_ref,
    cw_ref,
    cb_ref,
    hw_ref,
    hb_ref,
    gw_ref,
    gb_ref,
    gh_ref,
    ghb_ref,
    gf_ref,
    feat,
    wt,
    wn,
    wb,
    nat,
    xc,
    dc,
    dt,
    pre,
    gs,
    recv_a,
    send_b,
    recv_b,
    acc,
    s2,
    recv2,
    load,
    g_send,
    g_recv,
    a_send,
    a_recv,
    b_send,
    b_recv,
    r2_send,
    r2_recv,
):
    C = wt.shape[0]
    K3 = 3 * C
    K9 = 9 * C
    own = C // n_fsdp
    cells = rows * samples
    my_d = lax.axis_index("dp")
    my_f = lax.axis_index("fsdp")
    twin = my_f + 1 - 2 * lax.rem(my_f, 2)
    across = lax.rem(my_f + 2, 4)
    twin_across = lax.rem(twin + 2, 4)
    chunks = [pl.ds(0, K3), pl.ds(K3, K3), pl.ds(2 * K3, K3 + C)]

    def rows_of(f):
        return pl.ds(pl.multiple_of(f * own, own), own)

    mine = rows_of(my_f)

    def send(src, dst, send_sem, recv_sem, peer):
        copy = pltpu.make_async_remote_copy(
            src_ref=src,
            dst_ref=dst,
            send_sem=send_sem,
            recv_sem=recv_sem,
            device_id=peer,
            device_id_type=MESH,
        )
        copy.start()
        return copy

    load_kernel = pltpu.make_async_copy(cw_ref, wt.at[mine, pl.ds(0, K9)], load.at[0])
    load_features = pltpu.make_async_copy(feat_ref, feat, load.at[1])
    load_kernel.start()
    load_features.start()

    barrier = pltpu.get_barrier_semaphore()
    for f in (twin, across):
        pl.semaphore_signal(barrier, inc=1, device_id=(my_d, f), device_id_type=MESH)
    for k in range(1, n_dp):
        pl.semaphore_signal(
            barrier, inc=1, device_id=(lax.rem(my_d + k, n_dp), my_f), device_id_type=MESH
        )

    nat[...] = jnp.zeros_like(nat)
    nat[0:2, 0:own] = hw_ref[...].astype(f32)
    nat[2:3, 0:own] = cb_ref[...].astype(f32)
    wt[mine, K9 : K9 + C] = jnp.transpose(nat[...])[0:own, :].astype(bf16)
    pad = jnp.zeros((samples, K3), bf16)
    for ref in (xc, dc):
        ref[0:samples, :] = pad
        ref[(rows + 1) * samples : (rows + 2) * samples, :] = pad
    load_kernel.wait()

    pl.semaphore_wait(barrier, 2 + (n_dp - 1))

    sent = []
    gather_x, gather_t, gather_r = [], [], []
    for q in range(3):
        part = wt.at[mine, chunks[q]]
        gather_x.append(send(part, part, g_send.at[0, q], g_recv.at[0, q], (my_d, across)))
        gather_t.append(send(part, part, g_send.at[1, q], g_recv.at[1, q], (my_d, twin)))
    load_features.wait()

    spot = lax.broadcasted_iota(jnp.int32, (samples, C), 0)

    def shifts(wide):
        before = jnp.where(spot == 0, 0.0, pltpu.roll(wide, 1, 0))
        after = jnp.where(spot == samples - 1, 0.0, pltpu.roll(wide, samples - 1, 0))
        return before.astype(bf16), after.astype(bf16)

    for i in range(rows):
        at = slice((i + 1) * samples, (i + 2) * samples)
        block = feat[i * samples : (i + 1) * samples, :]
        before, after = shifts(block.astype(f32))
        xc[at, 0:C] = before
        xc[at, C : 2 * C] = block
        xc[at, 2 * C : K3] = after

    def relay(q):
        gather_x[q].wait_recv()
        part = wt.at[rows_of(across), chunks[q]]
        gather_r.append(send(part, part, g_send.at[2, q], g_recv.at[2, q], (my_d, twin)))

    relay(0)
    for a in range(3):
        if a < 2:
            relay(a + 1)
        gather_t[a].wait_recv()
        gather_r[a].wait_recv()
        for t in range(3 * a, 3 * a + 3):
            part = wt[:, t * C : (t + 1) * C]
            wb[t * C : (t + 1) * C, :] = part
            wn[t * C : (t + 1) * C, :] = jnp.transpose(part.astype(f32)).astype(bf16)
        term = jnp.dot(
            xc[a * samples : a * samples + cells, :],
            wn[a * K3 : (a + 1) * K3, :],
            preferred_element_type=f32,
        )
        pre[...] = term if a == 0 else pre[...] + term
    small = jnp.transpose(wt[:, K9 : K9 + C].astype(f32))
    head = small[0:16].astype(bf16)
    bias = small[2:3]

    sub = lax.broadcasted_iota(jnp.int32, (16, samples), 0)
    lane = lax.broadcasted_iota(jnp.int32, (16, samples), 1).astype(f32)
    head_bias = jnp.where(sub == 0, hb_ref[0], hb_ref[1])
    grad_head = jnp.zeros((16, C), f32)
    grad_hbias = jnp.zeros((16, samples), f32)
    grad_bias = jnp.zeros((1, C), f32)
    step = 2
    for i0 in range(0, rows, step):
        cut = slice(i0 * samples, (i0 + step) * samples)
        preact = pre[cut, :] + bias
        gate = jax.nn.sigmoid(preact)
        hidden = (preact * gate).astype(bf16)
        slope = gate * (1.0 + preact * (1.0 - gate))
        logits = lax.dot_general(head, hidden, NT, preferred_element_type=f32)
        dlogits = []
        for i in range(i0, i0 + step):
            arrival = jnp.where(sub == 0, pick_ref[0, i], pick_ref[1, i]).astype(f32)
            gap = lane - arrival
            target = jnp.exp(-(gap * gap) / (2.0 * SIGMA * SIGMA))
            usable = jnp.where(sub < 2, good_ref[0, i].astype(f32), 0.0)
            here = logits[:, (i - i0) * samples : (i - i0 + 1) * samples] + head_bias
            dlogits.append((usable * (jax.nn.sigmoid(here) - target)).astype(bf16))
            grad_hbias = grad_hbias + dlogits[-1].astype(f32)
        dlogit = jnp.concatenate(dlogits, axis=1)
        grad_head = grad_head + jnp.dot(dlogit, hidden, preferred_element_type=f32)
        dact = lax.dot_general(dlogit, head, TN, preferred_element_type=f32)
        dpre = (dact * slope).astype(bf16)
        wide = dpre.astype(f32)
        grad_bias = grad_bias + jnp.sum(wide, axis=0, keepdims=True)
        dt[:, cut] = jnp.transpose(wide).astype(bf16)
        for i in range(i0, i0 + step):
            inner = slice((i - i0) * samples, (i - i0 + 1) * samples)
            before, after = shifts(wide[inner])
            at = slice((i + 1) * samples, (i + 2) * samples)
            dc[at, 0:C] = after
            dc[at, C : 2 * C] = dpre[inner]
            dc[at, 2 * C : K3] = before

    def split(value):
        high = value.astype(bf16).astype(f32)
        return high, value - high

    def resplit(value):
        lanes = lax.broadcasted_iota(jnp.int32, value.shape, 1)
        high, low = split(value + pltpu.roll(value, value.shape[1] - AUX, 1))
        low = pltpu.roll(low, AUX, 1)
        return jnp.where(lanes < AUX, high, jnp.where(lanes < 2 * AUX, low, 0.0))

    first_a, first_b = [], []

    def stage_a(q):
        first_a.append(
            [
                send(
                    gs.at[rows_of(f), chunks[q]],
                    recv_a.at[j, :, chunks[q]],
                    a_send.at[j, q],
                    a_recv.at[j, q],
                    (my_d, twin),
                )
                for j, f in ((1, twin_across), (0, twin))
            ]
        )

    def stage_b(q):
        first_a[q][0].wait_recv()
        total = gs[rows_of(across), chunks[q]].astype(f32) + recv_a[1, :, chunks[q]].astype(f32)
        if q == 2:
            send_b[:, 2 * K3 : K9] = total[:, 0:K3].astype(bf16)
            send_b[:, K9 : K9 + C] = resplit(total[:, K3:]).astype(bf16)
        else:
            send_b[:, chunks[q]] = total.astype(bf16)
        part = send_b.at[:, chunks[q]]
        first_b.append(
            send(part, recv_b.at[:, chunks[q]], b_send.at[q], b_recv.at[q], (my_d, across))
        )

    def kernel_grads(a):
        grads = jnp.dot(
            dt[...], xc[a * samples : a * samples + cells, :], preferred_element_type=f32
        )
        gs[:, a * K3 : (a + 1) * K3] = grads.astype(bf16)

    def feature_grads(i):
        back = jnp.zeros((samples, C), f32)
        for a in range(3):
            back = back + jnp.dot(
                dc[(i + 2 - a) * samples : (i + 3 - a) * samples, :],
                wb[a * K3 : (a + 1) * K3, :],
                preferred_element_type=f32,
            )
        gf_ref[i * samples : (i + 1) * samples, :] = back.astype(bf16)

    hsum = jnp.sum(grad_hbias, axis=1, keepdims=True)
    sub8 = lax.broadcasted_iota(jnp.int32, (AUX, C), 0)
    rest = jnp.where(sub8 == 2, grad_bias, jnp.where(sub8 == 3, hsum[0:1], hsum[1:2]))
    rest = jnp.where(sub8 < 2, grad_head[0:AUX], jnp.where(sub8 < 5, rest, 0.0))
    high, low = split(rest)
    nat[...] = jnp.zeros_like(nat)
    nat[0:AUX, :] = high
    nat[AUX : 2 * AUX, :] = low
    gs[:, K9 : K9 + C] = jnp.transpose(nat[...]).astype(bf16)
    kernel_grads(0)
    stage_a(0)
    kernel_grads(1)
    stage_a(1)
    stage_b(0)
    kernel_grads(2)
    stage_a(2)
    stage_b(1)
    for i in range(rows // 2):
        feature_grads(i)
    stage_b(2)
    for i in range(rows // 2, rows):
        feature_grads(i)

    for q in range(3):
        first_a[q][1].wait_recv()
        first_b[q].wait_recv()
        acc[:, chunks[q]] = (
            gs[mine, chunks[q]].astype(f32)
            + recv_a[0, :, chunks[q]].astype(f32)
            + recv_b[:, chunks[q]].astype(f32)
        )
    acc[:, K9 + C :] = jnp.zeros((own, acc.shape[1] - K9 - C), f32)

    column = lax.broadcasted_iota(jnp.int32, (own, span), 1)
    small = pltpu.roll(resplit(acc[:, K9 : K9 + span]), owned, 1)
    for d in range(n_dp):
        base = owned * d // 128 * 128
        piece = acc[:, base : base + span + 128]
        if owned * d > base:
            piece = pltpu.roll(piece, span + 128 - (owned * d - base), 1)
        piece = jnp.where(column < owned, piece[:, 0:span], small)
        s2[d, 0:own, :] = piece[:, 0:128].astype(bf16)
        if span > 128:
            more = piece[:, 128:256]
            half = own // 2
            more = jnp.where(
                column[0:half, 0:128] < 64, more[0:half], pltpu.roll(more[half:], 64, 1)
            )
            s2[d, own : own + half, :] = more.astype(bf16)

    seconds = []
    for k in range(1, n_dp):
        peer = lax.rem(my_d + k, n_dp)
        seconds.append(
            send(s2.at[peer], recv2.at[k - 1], r2_send.at[k - 1], r2_recv.at[k - 1], (peer, my_f))
        )
    total = s2[my_d].astype(f32)
    for k in range(1, n_dp):
        seconds[k - 1].wait_recv()
        total = total + recv2[k - 1].astype(f32)
    if span > 128:
        more = total[own:]
        more = jnp.concatenate([more, pltpu.roll(more, 64, 1)], axis=0)
        total = jnp.concatenate([total[0:own], more], axis=1)
    gw_ref[...] = total[:, 0:owned]
    small = pltpu.roll(total, span - owned, 1)
    small = small + pltpu.roll(small, span - AUX, 1)
    nat[0:own, :] = small[:, 0:C]
    ghb_ref[...] = small[0:1, 3:5]
    turned = jnp.transpose(nat[...])
    gh_ref[...] = turned[0:2, 0:own]
    gb_ref[...] = turned[2:3, 0:own]

    for copies in [gather_x, gather_t, gather_r, *first_a, first_b, seconds]:
        for copy in copies:
            copy.wait_send()


def store_kernel(*refs):
    count = len(refs) // 2
    copies = [
        pltpu.make_async_copy(refs[i], refs[count + i], refs[-1].at[i]) for i in range(count)
    ]
    for copy in copies:
        copy.start()
    for copy in copies:
        copy.wait()


def on_device(n_dp, n_fsdp, features, pick_index, good_channel, conv_weight, conv_bias, head_weight, head_bias):
    _, rows, samples, C = features.shape
    cells = rows * samples
    K9 = conv_weight.shape[0]
    own = conv_weight.shape[1]
    owned = K9 // n_dp
    wire = own
    span = -(-(owned + 2 * AUX) // 128) * 128
    if span > 128:
        wire = own + own // 2
    vmem = pl.BlockSpec(memory_space=pltpu.VMEM)
    anywhere = pl.BlockSpec(memory_space=pl.ANY)
    hbm = pl.BlockSpec(memory_space=pltpu.HBM)
    smem = pl.BlockSpec(memory_space=pltpu.SMEM)
    dma = pltpu.SemaphoreType.DMA
    results = pl.pallas_call(
        functools.partial(kernel, n_dp, n_fsdp, rows, samples, owned, span),
        out_shape=(
            jax.ShapeDtypeStruct((own, owned), f32),
            jax.ShapeDtypeStruct((1, own), f32),
            jax.ShapeDtypeStruct((2, own), f32),
            jax.ShapeDtypeStruct((1, 2), f32),
            jax.ShapeDtypeStruct((cells, C), bf16),
        ),
        in_specs=[hbm, smem, smem, hbm, vmem, vmem, smem],
        out_specs=(vmem,) * 5,
        scratch_shapes=[
            pltpu.VMEM((cells, C), bf16),
            pltpu.VMEM((C, K9 + C), bf16),
            pltpu.VMEM((K9, C), bf16),
            pltpu.VMEM((K9, C), bf16),
            pltpu.VMEM((C, C), f32),
            pltpu.VMEM(((rows + 2) * samples, 3 * C), bf16),
            pltpu.VMEM(((rows + 2) * samples, 3 * C), bf16),
            pltpu.VMEM((C, cells), bf16),
            pltpu.VMEM((cells, C), f32),
            pltpu.VMEM((C, K9 + C), bf16),
            pltpu.VMEM((2, own, K9 + C), bf16),
            pltpu.VMEM((own, K9 + C), bf16),
            pltpu.VMEM((own, K9 + C), bf16),
            pltpu.VMEM((own, K9 + span + 128), f32),
            pltpu.VMEM((n_dp, wire, 128), bf16),
            pltpu.VMEM((n_dp - 1, wire, 128), bf16),
            dma((2,)),
            dma((3, 3)),
            dma((3, 3)),
            dma((2, 3)),
            dma((2, 3)),
            dma((3,)),
            dma((3,)),
            dma((n_dp - 1,)),
            dma((n_dp - 1,)),
        ],
        compiler_params=pltpu.CompilerParams(
            collective_id=0, has_side_effects=True, vmem_limit_bytes=48 * 1024 * 1024
        ),
        cost_estimate=pl.CostEstimate(
            flops=6 * cells * K9 * C, bytes_accessed=4 * cells * C, transcendentals=2 * cells * C
        ),
    )(
        features.reshape(cells, C),
        jnp.transpose(pick_index[0]),
        good_channel,
        jnp.transpose(conv_weight),
        conv_bias,
        head_weight,
        head_bias,
    )
    gw, gb, gh, ghb, gf = pl.pallas_call(
        store_kernel,
        out_shape=tuple(jax.ShapeDtypeStruct(r.shape, r.dtype) for r in results),
        in_specs=[anywhere] * 5,
        out_specs=(hbm,) * 5,
        scratch_shapes=[dma((5,))],
        compiler_params=pltpu.CompilerParams(vmem_limit_bytes=1024 * 1024),
    )(*results)
    return jnp.transpose(gw), gb, gh, ghb.reshape(2), gf.reshape(features.shape)


def solution(mesh):
    return jax.shard_map(
        functools.partial(on_device, mesh.shape["dp"], mesh.shape["fsdp"]),
        mesh=mesh,
        in_specs=(
            P(("dp", "fsdp"), None, None, None),
            P(("dp", "fsdp"), None, None),
            P(("dp", "fsdp"), None),
            P(None, "fsdp"),
            P(None, "fsdp"),
            P(None, "fsdp"),
            P(),
        ),
        out_specs=(
            P("dp", "fsdp"),
            P(None, "fsdp"),
            P(None, "fsdp"),
            P(),
            P(("dp", "fsdp"), None, None, None),
        ),
        check_vma=False,
    )
```

```python
import functools

import jax
import jax.numpy as jnp
from jax import lax
from jax.experimental import pallas as pl
from jax.experimental.pallas import tpu as pltpu
from jax.sharding import PartitionSpec as P

SIGMA = 20
MESH = pl.DeviceIdType.MESH
AUX = 8
NT = (((1,), (1,)), ((), ()))
TN = (((0,), (0,)), ((), ()))
f32 = jnp.float32
bf16 = jnp.bfloat16


def kernel(
    n_dp,
    n_fsdp,
    rows,
    samples,
    owned,
    span,
    feat_ref,
    pick_ref,
    good_ref,
    cw_ref,
    cb_ref,
    hw_ref,
    hb_ref,
    gw_ref,
    gb_ref,
    gh_ref,
    ghb_ref,
    gf_ref,
    feat,
    wt,
    wn,
    wb,
    nat,
    xc,
    dc,
    dt,
    pre,
    gs,
    recv_a,
    send_b,
    recv_b,
    acc,
    s2,
    recv2,
    load,
    g_send,
    g_recv,
    a_send,
    a_recv,
    b_send,
    b_recv,
    r2_send,
    r2_recv,
):
    C = wt.shape[0]
    K3 = 3 * C
    K9 = 9 * C
    own = C // n_fsdp
    cells = rows * samples
    my_d = lax.axis_index("dp")
    my_f = lax.axis_index("fsdp")
    twin = my_f + 1 - 2 * lax.rem(my_f, 2)
    across = lax.rem(my_f + 2, 4)
    twin_across = lax.rem(twin + 2, 4)
    chunks = [pl.ds(0, K3), pl.ds(K3, K3), pl.ds(2 * K3, K3 + C)]

    def rows_of(f):
        return pl.ds(pl.multiple_of(f * own, own), own)

    mine = rows_of(my_f)

    def send(src, dst, send_sem, recv_sem, peer):
        copy = pltpu.make_async_remote_copy(
            src_ref=src,
            dst_ref=dst,
            send_sem=send_sem,
            recv_sem=recv_sem,
            device_id=peer,
            device_id_type=MESH,
        )
        copy.start()
        return copy

    load_kernel = pltpu.make_async_copy(cw_ref, wt.at[mine, pl.ds(0, K9)], load.at[0])
    load_features = pltpu.make_async_copy(feat_ref, feat, load.at[1])
    load_kernel.start()
    load_features.start()

    barrier = pltpu.get_barrier_semaphore()
    for f in (twin, across):
        pl.semaphore_signal(barrier, inc=1, device_id=(my_d, f), device_id_type=MESH)
    for k in range(1, n_dp):
        pl.semaphore_signal(
            barrier, inc=1, device_id=(lax.rem(my_d + k, n_dp), my_f), device_id_type=MESH
        )

    nat[...] = jnp.zeros_like(nat)
    nat[0:2, 0:own] = hw_ref[...].astype(f32)
    nat[2:3, 0:own] = cb_ref[...].astype(f32)
    wt[mine, K9 : K9 + C] = jnp.transpose(nat[...])[0:own, :].astype(bf16)
    pad = jnp.zeros((samples, K3), bf16)
    for ref in (xc, dc):
        ref[0:samples, :] = pad
        ref[(rows + 1) * samples : (rows + 2) * samples, :] = pad
    load_kernel.wait()

    pl.semaphore_wait(barrier, 2 + (n_dp - 1))

    sent = []
    gather_x, gather_t, gather_r = [], [], []
    for q in range(3):
        part = wt.at[mine, chunks[q]]
        gather_x.append(send(part, part, g_send.at[0, q], g_recv.at[0, q], (my_d, across)))
        gather_t.append(send(part, part, g_send.at[1, q], g_recv.at[1, q], (my_d, twin)))
    load_features.wait()

    spot = lax.broadcasted_iota(jnp.int32, (samples, C), 0)

    def shifts(wide):
        before = jnp.where(spot == 0, 0.0, pltpu.roll(wide, 1, 0))
        after = jnp.where(spot == samples - 1, 0.0, pltpu.roll(wide, samples - 1, 0))
        return before.astype(bf16), after.astype(bf16)

    for i in range(rows):
        at = slice((i + 1) * samples, (i + 2) * samples)
        block = feat[i * samples : (i + 1) * samples, :]
        before, after = shifts(block.astype(f32))
        xc[at, 0:C] = before
        xc[at, C : 2 * C] = block
        xc[at, 2 * C : K3] = after

    def relay(q):
        gather_x[q].wait_recv()
        part = wt.at[rows_of(across), chunks[q]]
        gather_r.append(send(part, part, g_send.at[2, q], g_recv.at[2, q], (my_d, twin)))

    relay(0)
    for a in range(3):
        if a < 2:
            relay(a + 1)
        gather_t[a].wait_recv()
        gather_r[a].wait_recv()
        for t in range(3 * a, 3 * a + 3):
            part = wt[:, t * C : (t + 1) * C]
            wb[t * C : (t + 1) * C, :] = part
            wn[t * C : (t + 1) * C, :] = jnp.transpose(part.astype(f32)).astype(bf16)
        term = jnp.dot(
            xc[a * samples : a * samples + cells, :],
            wn[a * K3 : (a + 1) * K3, :],
            preferred_element_type=f32,
        )
        pre[...] = term if a == 0 else pre[...] + term
    small = jnp.transpose(wt[:, K9 : K9 + C].astype(f32))
    head = small[0:16].astype(bf16)
    bias = small[2:3]

    sub = lax.broadcasted_iota(jnp.int32, (16, samples), 0)
    lane = lax.broadcasted_iota(jnp.int32, (16, samples), 1).astype(f32)
    head_bias = jnp.where(sub == 0, hb_ref[0], hb_ref[1])
    grad_head = jnp.zeros((16, C), f32)
    grad_hbias = jnp.zeros((16, samples), f32)
    grad_bias = jnp.zeros((1, C), f32)
    step = 2
    for i0 in range(0, rows, step):
        cut = slice(i0 * samples, (i0 + step) * samples)
        preact = pre[cut, :] + bias
        gate = jax.nn.sigmoid(preact)
        hidden = (preact * gate).astype(bf16)
        slope = gate * (1.0 + preact * (1.0 - gate))
        logits = lax.dot_general(head, hidden, NT, preferred_element_type=f32)
        dlogits = []
        for i in range(i0, i0 + step):
            arrival = jnp.where(sub == 0, pick_ref[0, i], pick_ref[1, i]).astype(f32)
            gap = lane - arrival
            target = jnp.exp(-(gap * gap) / (2.0 * SIGMA * SIGMA))
            usable = jnp.where(sub < 2, good_ref[0, i].astype(f32), 0.0)
            here = logits[:, (i - i0) * samples : (i - i0 + 1) * samples] + head_bias
            dlogits.append((usable * (jax.nn.sigmoid(here) - target)).astype(bf16))
            grad_hbias = grad_hbias + dlogits[-1].astype(f32)
        dlogit = jnp.concatenate(dlogits, axis=1)
        grad_head = grad_head + jnp.dot(dlogit, hidden, preferred_element_type=f32)
        dact = lax.dot_general(dlogit, head, TN, preferred_element_type=f32)
        dpre = (dact * slope).astype(bf16)
        wide = dpre.astype(f32)
        grad_bias = grad_bias + jnp.sum(wide, axis=0, keepdims=True)
        dt[:, cut] = jnp.transpose(wide).astype(bf16)
        for i in range(i0, i0 + step):
            inner = slice((i - i0) * samples, (i - i0 + 1) * samples)
            before, after = shifts(wide[inner])
            at = slice((i + 1) * samples, (i + 2) * samples)
            dc[at, 0:C] = after
            dc[at, C : 2 * C] = dpre[inner]
            dc[at, 2 * C : K3] = before

    def split(value):
        high = value.astype(bf16).astype(f32)
        return high, value - high

    def resplit(value):
        lanes = lax.broadcasted_iota(jnp.int32, value.shape, 1)
        high, low = split(value + pltpu.roll(value, value.shape[1] - AUX, 1))
        low = pltpu.roll(low, AUX, 1)
        return jnp.where(lanes < AUX, high, jnp.where(lanes < 2 * AUX, low, 0.0))

    first_a, first_b = [], []

    def stage_a(q):
        first_a.append(
            [
                send(
                    gs.at[rows_of(f), chunks[q]],
                    recv_a.at[j, :, chunks[q]],
                    a_send.at[j, q],
                    a_recv.at[j, q],
                    (my_d, twin),
                )
                for j, f in ((1, twin_across), (0, twin))
            ]
        )

    def stage_b(q):
        first_a[q][0].wait_recv()
        total = gs[rows_of(across), chunks[q]].astype(f32) + recv_a[1, :, chunks[q]].astype(f32)
        if q == 2:
            send_b[:, 2 * K3 : K9] = total[:, 0:K3].astype(bf16)
            send_b[:, K9 : K9 + C] = resplit(total[:, K3:]).astype(bf16)
        else:
            send_b[:, chunks[q]] = total.astype(bf16)
        part = send_b.at[:, chunks[q]]
        first_b.append(
            send(part, recv_b.at[:, chunks[q]], b_send.at[q], b_recv.at[q], (my_d, across))
        )

    def kernel_grads(a):
        grads = jnp.dot(
            dt[...], xc[a * samples : a * samples + cells, :], preferred_element_type=f32
        )
        gs[:, a * K3 : (a + 1) * K3] = grads.astype(bf16)

    def feature_grads(i):
        back = jnp.zeros((samples, C), f32)
        for a in range(3):
            back = back + jnp.dot(
                dc[(i + 2 - a) * samples : (i + 3 - a) * samples, :],
                wb[a * K3 : (a + 1) * K3, :],
                preferred_element_type=f32,
            )
        gf_ref[i * samples : (i + 1) * samples, :] = back.astype(bf16)

    hsum = jnp.sum(grad_hbias, axis=1, keepdims=True)
    sub8 = lax.broadcasted_iota(jnp.int32, (AUX, C), 0)
    rest = jnp.where(sub8 == 2, grad_bias, jnp.where(sub8 == 3, hsum[0:1], hsum[1:2]))
    rest = jnp.where(sub8 < 2, grad_head[0:AUX], jnp.where(sub8 < 5, rest, 0.0))
    high, low = split(rest)
    nat[...] = jnp.zeros_like(nat)
    nat[0:AUX, :] = high
    nat[AUX : 2 * AUX, :] = low
    gs[:, K9 : K9 + C] = jnp.transpose(nat[...]).astype(bf16)
    kernel_grads(0)
    stage_a(0)
    kernel_grads(1)
    stage_a(1)
    stage_b(0)
    kernel_grads(2)
    stage_a(2)
    stage_b(1)
    for i in range(rows // 2):
        feature_grads(i)
    stage_b(2)
    for i in range(rows // 2, rows):
        feature_grads(i)

    for q in range(3):
        first_a[q][1].wait_recv()
        first_b[q].wait_recv()
        acc[:, chunks[q]] = (
            gs[mine, chunks[q]].astype(f32)
            + recv_a[0, :, chunks[q]].astype(f32)
            + recv_b[:, chunks[q]].astype(f32)
        )
    acc[:, K9 + C :] = jnp.zeros((own, acc.shape[1] - K9 - C), f32)

    column = lax.broadcasted_iota(jnp.int32, (own, span), 1)
    small = pltpu.roll(resplit(acc[:, K9 : K9 + span]), owned, 1)
    for d in range(n_dp):
        base = owned * d // 128 * 128
        piece = acc[:, base : base + span + 128]
        if owned * d > base:
            piece = pltpu.roll(piece, span + 128 - (owned * d - base), 1)
        piece = jnp.where(column < owned, piece[:, 0:span], small)
        s2[d, 0:own, :] = piece[:, 0:128].astype(bf16)
        if span > 128:
            more = piece[:, 128:256]
            half = own // 2
            more = jnp.where(
                column[0:half, 0:128] < 64, more[0:half], pltpu.roll(more[half:], 64, 1)
            )
            s2[d, own : own + half, :] = more.astype(bf16)

    seconds = []
    for k in range(1, n_dp):
        peer = lax.rem(my_d + k, n_dp)
        seconds.append(
            send(s2.at[peer], recv2.at[k - 1], r2_send.at[k - 1], r2_recv.at[k - 1], (peer, my_f))
        )
    total = s2[my_d].astype(f32)
    for k in range(1, n_dp):
        seconds[k - 1].wait_recv()
        total = total + recv2[k - 1].astype(f32)
    if span > 128:
        more = total[own:]
        more = jnp.concatenate([more, pltpu.roll(more, 64, 1)], axis=0)
        total = jnp.concatenate([total[0:own], more], axis=1)
    gw_ref[...] = total[:, 0:owned]
    small = pltpu.roll(total, span - owned, 1)
    small = small + pltpu.roll(small, span - AUX, 1)
    nat[0:own, :] = small[:, 0:C]
    ghb_ref[...] = small[0:1, 3:5]
    turned = jnp.transpose(nat[...])
    gh_ref[...] = turned[0:2, 0:own]
    gb_ref[...] = turned[2:3, 0:own]

    for copies in [gather_x, gather_t, gather_r, *first_a, first_b, seconds]:
        for copy in copies:
            copy.wait_send()


def store_kernel(*refs):
    count = len(refs) // 2
    copies = [
        pltpu.make_async_copy(refs[i], refs[count + i], refs[-1].at[i]) for i in range(count)
    ]
    for copy in copies:
        copy.start()
    for copy in copies:
        copy.wait()


def on_device(n_dp, n_fsdp, features, pick_index, good_channel, conv_weight, conv_bias, head_weight, head_bias):
    _, rows, samples, C = features.shape
    cells = rows * samples
    K9 = conv_weight.shape[0]
    own = conv_weight.shape[1]
    owned = K9 // n_dp
    wire = own
    span = -(-(owned + 2 * AUX) // 128) * 128
    if span > 128:
        wire = own + own // 2
    vmem = pl.BlockSpec(memory_space=pltpu.VMEM)
    anywhere = pl.BlockSpec(memory_space=pl.ANY)
    hbm = pl.BlockSpec(memory_space=pltpu.HBM)
    smem = pl.BlockSpec(memory_space=pltpu.SMEM)
    dma = pltpu.SemaphoreType.DMA
    results = pl.pallas_call(
        functools.partial(kernel, n_dp, n_fsdp, rows, samples, owned, span),
        out_shape=(
            jax.ShapeDtypeStruct((own, owned), f32),
            jax.ShapeDtypeStruct((1, own), f32),
            jax.ShapeDtypeStruct((2, own), f32),
            jax.ShapeDtypeStruct((1, 2), f32),
            jax.ShapeDtypeStruct((cells, C), bf16),
        ),
        in_specs=[hbm, smem, smem, hbm, vmem, vmem, smem],
        out_specs=(vmem,) * 5,
        scratch_shapes=[
            pltpu.VMEM((cells, C), bf16),
            pltpu.VMEM((C, K9 + C), bf16),
            pltpu.VMEM((K9, C), bf16),
            pltpu.VMEM((K9, C), bf16),
            pltpu.VMEM((C, C), f32),
            pltpu.VMEM(((rows + 2) * samples, 3 * C), bf16),
            pltpu.VMEM(((rows + 2) * samples, 3 * C), bf16),
            pltpu.VMEM((C, cells), bf16),
            pltpu.VMEM((cells, C), f32),
            pltpu.VMEM((C, K9 + C), bf16),
            pltpu.VMEM((2, own, K9 + C), bf16),
            pltpu.VMEM((own, K9 + C), bf16),
            pltpu.VMEM((own, K9 + C), bf16),
            pltpu.VMEM((own, K9 + span + 128), f32),
            pltpu.VMEM((n_dp, wire, 128), bf16),
            pltpu.VMEM((n_dp - 1, wire, 128), bf16),
            dma((2,)),
            dma((3, 3)),
            dma((3, 3)),
            dma((2, 3)),
            dma((2, 3)),
            dma((3,)),
            dma((3,)),
            dma((n_dp - 1,)),
            dma((n_dp - 1,)),
        ],
        compiler_params=pltpu.CompilerParams(
            collective_id=0, has_side_effects=True, vmem_limit_bytes=48 * 1024 * 1024
        ),
        cost_estimate=pl.CostEstimate(
            flops=6 * cells * K9 * C, bytes_accessed=4 * cells * C, transcendentals=2 * cells * C
        ),
    )(
        pltpu.with_memory_space_constraint(features.reshape(cells, C), pltpu.HBM),
        jnp.transpose(pick_index[0]),
        good_channel,
        pltpu.with_memory_space_constraint(jnp.transpose(conv_weight), pltpu.HBM),
        conv_bias,
        head_weight,
        head_bias,
    )
    gw, gb, gh, ghb, gf = pl.pallas_call(
        store_kernel,
        out_shape=tuple(jax.ShapeDtypeStruct(r.shape, r.dtype) for r in results),
        in_specs=[anywhere] * 5,
        out_specs=(hbm,) * 5,
        scratch_shapes=[dma((5,))],
        compiler_params=pltpu.CompilerParams(vmem_limit_bytes=1024 * 1024),
    )(*results)
    return jnp.transpose(gw), gb, gh, ghb.reshape(2), gf.reshape(features.shape)


def solution(mesh):
    return jax.shard_map(
        functools.partial(on_device, mesh.shape["dp"], mesh.shape["fsdp"]),
        mesh=mesh,
        in_specs=(
            P(("dp", "fsdp"), None, None, None),
            P(("dp", "fsdp"), None, None),
            P(("dp", "fsdp"), None),
            P(None, "fsdp"),
            P(None, "fsdp"),
            P(None, "fsdp"),
            P(),
        ),
        out_specs=(
            P("dp", "fsdp"),
            P(None, "fsdp"),
            P(None, "fsdp"),
            P(),
            P(("dp", "fsdp"), None, None, None),
        ),
        check_vma=False,
    )
```
